256 devices in a mesh: rowa: 32 (over x_lo, z, core), rowb: 8 (over x_hi, y).
Axes of the slice: x: 4 (x_hi: 2, x_lo: 2; x = x_hi * 2 + x_lo), y: 4, z: 8, core: 2. Of those that a mesh axis runs over, the one named last changes fastest.
Arguments:
- corpus: bfloat16 [196608, 4096], P(('rowa', 'rowb')), may hold values from -240 to 240
- sketch: bfloat16 [4096, 256], replicated, may hold values from -0.09375 to 0.09375
Outputs:
- basis: float32 [196608, 256], P(('rowa', 'rowb'))
- projected: float32 [256, 4096], replicated
The draws below stay inside these ranges and needn't reach their ends.
All inputs are finite; a program needn't handle non-finite values.
Results may differ from the reference program's by a relative error of at most 0.0003.
Values sent between devices are 32-bit elements; how exact they have to be, the bound alone decides.
No kernel may reach another device: no remote copies, remote signals or barrier semaphores. Data moves between devices by JAX's collectives and lax.ppermute only.
A program may use at most 64 MiB of HBM per device.

```python
import jax
import jax.numpy as jnp
from jax import lax

D = 4096
K = 256
ROWS_DEV = 768
ROWS = 196608


def draw_corpus(key, part):
    key = jax.random.fold_in(key, 11)
    first, second, third = jax.random.split(key, 3)
    positions = jnp.arange(ROWS, dtype=jnp.float32)
    rising = jnp.exp(jnp.log(3.0) * positions / ROWS)
    base = jnp.clip(jax.random.normal(first, (ROWS, D), jnp.float32), -4.0, 4.0)
    row_scale = jnp.exp(jax.random.uniform(second, (ROWS, 1), jnp.float32) * jnp.log(10.0))
    col_scale = jnp.exp(jax.random.uniform(third, (1, D), jnp.float32, -jnp.log(2.0), jnp.log(2.0)))
    return (base * row_scale * rising[:, None] * col_scale).astype(jnp.bfloat16)


def gaussian(own_key, shape, width, limit, held_as=jnp.bfloat16):
    return jnp.clip(width * jax.random.normal(own_key, shape, jnp.float32), -limit, limit).astype(held_as)


def setup_inputs(seed: int = 0) -> dict:
    key_list = jax.random.split(jax.random.key(seed), 3)
    return {
        "corpus": draw_corpus(jax.random.fold_in(key_list[2], 71), 0),
        "sketch": gaussian(key_list[1], (D, K), D ** -0.5, 0.09375),
    }


def reference(corpus, sketch):
    sampled = jnp.dot(corpus.astype(jnp.float32), sketch.astype(jnp.float32), preferred_element_type=jnp.float32)
    gram = jnp.dot(sampled.T, sampled, precision=lax.Precision.HIGHEST) / ROWS
    lower = jnp.linalg.cholesky(gram)
    basis_t = jax.scipy.linalg.solve_triangular(lower, sampled.T, lower=True)
    basis = basis_t.T
    blocks = ROWS // ROWS_DEV
    corpus_blocks = corpus.reshape(blocks, ROWS_DEV, D)
    basis_blocks = basis.reshape(blocks, ROWS_DEV, K)

    def step(total, pair):
        rows_c, rows_b = pair
        part_sum = jnp.dot(rows_b.T, rows_c.astype(jnp.float32), precision=lax.Precision.HIGHEST)
        return (total + part_sum, None)
    total, _ = lax.scan(step, jnp.zeros((K, D), jnp.float32), (corpus_blocks, basis_blocks))
    projected = total / jnp.sqrt(jnp.float32(ROWS))
    return (basis, projected)
```

```python
import functools

import jax
import jax.numpy as jnp
from jax import lax
from jax.experimental import pallas as pl
from jax.experimental.pallas import tpu as pltpu
from jax.sharding import PartitionSpec as P

AXES = ("rowa", "rowb")
D = 4096
K = 256
ROWS_DEV = 768
ROWS = 196608
NX, NY, NZ = 4, 4, 8
F32 = jnp.float32
BF16 = jnp.bfloat16
PIECE = 136
PARAMS = pltpu.CompilerParams(vmem_limit_bytes=48 * 1024 * 1024)


def index_of(x, y, z, core):
    return ((x % 2) * 16 + z * 2 + core) * 8 + (x // 2) * 4 + y


def shift(value, x=0, y=0, z=0, core=0):
    pairs = [
        (index_of(i, j, k, c), index_of((i + x) % NX, (j + y) % NY, (k + z) % NZ, (c + core) % 2))
        for i in range(NX)
        for j in range(NY)
        for k in range(NZ)
        for c in range(2)
    ]
    return lax.ppermute(value, AXES, pairs)


def own_bits():
    a, b = lax.axis_index("rowa"), lax.axis_index("rowb")
    core = a % 2
    parities = (a // 16) * 4 + (b % 2) * 2 + (a // 2) % 2
    upper = (b // 4) * 2 + (b // 2) % 2
    return jnp.stack([core, parities, upper]).astype(jnp.int32)


def split(value):
    high = value.astype(BF16)
    return high, (value - high.astype(F32)).astype(BF16)


def sketch_kernel(corpus_ref, sketch_ref, sampled_ref, high_ref, low_ref, gram_ref):
    sampled = jnp.dot(corpus_ref[...], sketch_ref[...], preferred_element_type=F32)
    sampled_ref[...] = sampled
    turned = sampled.T
    high, low = split(turned)
    high_ref[...] = high
    low_ref[...] = low
    gram = jnp.dot(turned, sampled, precision=lax.Precision.HIGHEST, preferred_element_type=F32)

    @pl.when(pl.program_id(0) == 0)
    def _():
        gram_ref[...] = gram

    @pl.when(pl.program_id(0) != 0)
    def _():
        gram_ref[...] += gram


def sketch_rows(corpus, sketch, step=256):
    return pl.pallas_call(
        sketch_kernel,
        grid=(ROWS_DEV // step,),
        in_specs=[
            pl.BlockSpec((step, D), lambda i: (i, 0)),
            pl.BlockSpec((D, K), lambda i: (0, 0)),
        ],
        out_specs=[
            pl.BlockSpec((step, K), lambda i: (i, 0)),
            pl.BlockSpec((K, step), lambda i: (0, i)),
            pl.BlockSpec((K, step), lambda i: (0, i)),
            pl.BlockSpec((K, K), lambda i: (0, 0)),
        ],
        out_shape=[
            jax.ShapeDtypeStruct((ROWS_DEV, K), F32),
            jax.ShapeDtypeStruct((K, ROWS_DEV), BF16),
            jax.ShapeDtypeStruct((K, ROWS_DEV), BF16),
            jax.ShapeDtypeStruct((K, K), F32),
        ],
        compiler_params=PARAMS,
        cost_estimate=pl.CostEstimate(
            flops=2 * ROWS_DEV * D * K, bytes_accessed=9_000_000, transcendentals=0
        ),
        name="sketch_rows",
    )(corpus, sketch)


def correlate_kernel(bits_ref, corpus_ref, high_ref, low_ref, gram_ref, out_ref):
    piece = pl.program_id(0) ^ bits_ref[1]
    block = corpus_ref[...]
    part = jnp.dot(high_ref[...], block, preferred_element_type=F32)
    part += jnp.dot(low_ref[...], block, preferred_element_type=F32)
    for q in range(4):
        out_ref[0, q, 0:64, :] = part[64 * q : 64 * q + 64, 0:128]
        out_ref[0, q, 64:128, :] = part[64 * q : 64 * q + 64, 128:256]
        row = pl.multiple_of(piece * 32 + q * 8, 8)
        out_ref[0, q, 128:136, :] = gram_ref[pl.ds(row, 8), :]


def correlate(bits, corpus, high, low, gram, flip):
    return pl.pallas_call(
        correlate_kernel,
        grid_spec=pltpu.PrefetchScalarGridSpec(
            num_scalar_prefetch=1,
            grid=(8,),
            in_specs=[
                pl.BlockSpec((ROWS_DEV, 256), lambda r, bits: (0, (bits[0] ^ flip) * 8 + (r ^ bits[1]))),
                pl.BlockSpec((K, ROWS_DEV), lambda r, bits: (0, 0)),
                pl.BlockSpec((K, ROWS_DEV), lambda r, bits: (0, 0)),
                pl.BlockSpec((K, 128), lambda r, bits: (0, bits[0] ^ flip)),
            ],
            out_specs=pl.BlockSpec((1, 4, PIECE, 128), lambda r, bits: (r, 0, 0, 0)),
        ),
        out_shape=jax.ShapeDtypeStruct((8, 4, PIECE, 128), F32),
        compiler_params=PARAMS,
        cost_estimate=pl.CostEstimate(
            flops=2 * ROWS_DEV * D * K, bytes_accessed=6_000_000, transcendentals=0
        ),
        name=f"correlate{flip}",
    )(bits, corpus, high, low, gram)


def leave_kernel(bits_ref, near_ref, ahead_ref, back_ref, *out_refs):
    for q in range(4):
        received = ahead_ref[q] if q < 2 else back_ref[q - 2]
        for apart in range(4):

            @pl.when(bits_ref[2] == q ^ apart)
            def _(q=q, apart=apart, received=received):
                out_refs[apart][...] = near_ref[q] + received


def leave_parts(bits, near, ahead, back):
    part = jax.ShapeDtypeStruct((PIECE, 128), F32)
    return pl.pallas_call(
        leave_kernel,
        grid_spec=pltpu.PrefetchScalarGridSpec(
            num_scalar_prefetch=1,
            grid=(),
            in_specs=[pl.BlockSpec(memory_space=pltpu.VMEM)] * 3,
            out_specs=[pl.BlockSpec(memory_space=pltpu.VMEM)] * 4,
        ),
        out_shape=[part] * 4,
        compiler_params=PARAMS,
        name="leave_parts",
    )(bits, near, ahead, back)


def join_kernel(bits_ref, *refs):
    for apart in range(4):
        refs[4][bits_ref[2] ^ apart] = refs[apart][...]


def join_parts(bits, parts):
    return pl.pallas_call(
        join_kernel,
        grid_spec=pltpu.PrefetchScalarGridSpec(
            num_scalar_prefetch=1,
            grid=(),
            in_specs=[pl.BlockSpec(memory_space=pltpu.VMEM)] * 4,
            out_specs=pl.BlockSpec(memory_space=pltpu.VMEM),
        ),
        out_shape=jax.ShapeDtypeStruct((4, PIECE, 128), F32),
        compiler_params=PARAMS,
        name="join_parts",
    )(bits, *parts)


def eliminate(panel, start):
    size = panel.shape[0]
    rows = lax.broadcasted_iota(jnp.int32, (size, 1), 0)
    lanes = lax.broadcasted_iota(jnp.int32, (1, K), 1)
    scale = jnp.ones((size, 1), F32)
    for j in range(size):
        column = panel[:, start + j : start + j + 1]
        pivot = column[j : j + 1, :]
        row = panel[j : j + 1, :]
        here = lanes == start + j
        factor = jnp.where(rows > j, column / pivot, 0.0)
        scale = jnp.where(rows == j, lax.rsqrt(pivot), scale)
        kept = jnp.where(jnp.logical_and(here, rows >= j), jnp.where(rows == j, 1.0, 0.0), panel)
        panel = kept - factor * jnp.where(here, 1.0, row)
    return panel * scale


def factor_kernel(bits_ref, near_ref, far_ref, other_ref, out_ref, half_ref, work_ref):
    for r in range(8):
        for q in range(4):
            row = pl.multiple_of((r ^ bits_ref[1]) * 32 + q * 8, 8)
            own = near_ref[r, q] if r < 4 else far_ref[r - 4, q]
            half_ref[bits_ref[0], pl.ds(row, 8), :] = own
            half_ref[1 - bits_ref[0], pl.ds(row, 8), :] = other_ref[r, q]
    work_ref[:, 0:128] = half_ref[0] / ROWS
    work_ref[:, 128:256] = half_ref[1] / ROWS
    step = 32
    lanes = lax.broadcasted_iota(jnp.int32, (1, K), 1)
    rows = lax.broadcasted_iota(jnp.int32, (step, 1), 0)
    for start in range(0, K, step):
        panel = eliminate(work_ref[start : start + step, :], start)
        work_ref[start : start + step, :] = panel
        end = start + step
        if end < K:
            own = jnp.logical_and(lanes >= start, lanes < end)
            masked = jnp.where(jnp.logical_and(own, lanes - start > rows), 0.0, panel)
            update = lax.dot_general(
                panel[:, end:],
                masked,
                (((0,), (0,)), ((), ())),
                precision=lax.Precision.HIGHEST,
                preferred_element_type=F32,
            )
            work_ref[end:, :] = jnp.where(own, 0.0, work_ref[end:, :]) - update
    down = lax.broadcasted_iota(jnp.int32, (K, K), 0)
    across = lax.broadcasted_iota(jnp.int32, (K, K), 1)
    out_ref[...] = jnp.where(down >= across, work_ref[...], 0.0)


def inverse_factor(bits, near, far, other):
    return pl.pallas_call(
        factor_kernel,
        grid_spec=pltpu.PrefetchScalarGridSpec(
            num_scalar_prefetch=1,
            grid=(),
            in_specs=[pl.BlockSpec(memory_space=pltpu.VMEM)] * 3,
            out_specs=pl.BlockSpec(memory_space=pltpu.VMEM),
            scratch_shapes=[pltpu.VMEM((2, K, 128), F32), pltpu.VMEM((K, K), F32)],
        ),
        out_shape=jax.ShapeDtypeStruct((K, K), F32),
        compiler_params=PARAMS,
        cost_estimate=pl.CostEstimate(
            flops=20_000_000_000, bytes_accessed=1_000_000, transcendentals=0
        ),
        name="inverse_factor",
    )(bits, near, far, other)


def basis_kernel(sampled_ref, inverse_ref, out_ref):
    out_ref[...] = lax.dot_general(
        sampled_ref[...],
        inverse_ref[...],
        (((1,), (1,)), ((), ())),
        precision=lax.Precision.HIGHEST,
        preferred_element_type=F32,
    )


def basis_rows(sampled, inverse, step=256):
    return pl.pallas_call(
        basis_kernel,
        grid=(ROWS_DEV // step,),
        in_specs=[
            pl.BlockSpec((step, K), lambda i: (i, 0)),
            pl.BlockSpec((K, K), lambda i: (0, 0)),
        ],
        out_specs=pl.BlockSpec((step, K), lambda i: (i, 0)),
        out_shape=jax.ShapeDtypeStruct((ROWS_DEV, K), F32),
        compiler_params=PARAMS,
        cost_estimate=pl.CostEstimate(
            flops=6 * 2 * ROWS_DEV * K * K, bytes_accessed=2_000_000, transcendentals=0
        ),
        name="basis_rows",
    )(sampled, inverse)


def project_kernel(bits_ref, inverse_ref, *refs):
    sources, (out_ref, work_ref) = refs[:-2], refs[-2:]
    step = pl.program_id(0)
    begin = 0
    for source in sources:
        count = 4 if source is sources[0] or source is sources[3] else 2
        begins = begin

        @pl.when(jnp.logical_and(step >= begins, step < begins + count))
        def _(source=source):
            for q in range(4):
                work_ref[64 * q : 64 * q + 64, 0:128] = source[0, q, 0:64, :]
                work_ref[64 * q : 64 * q + 64, 128:256] = source[0, q, 64:128, :]

        begin += count
    inverse_high, inverse_low = split(inverse_ref[...])
    high, low = split(work_ref[...])
    total = jnp.dot(inverse_high, low, preferred_element_type=F32)
    total += jnp.dot(inverse_low, high, preferred_element_type=F32)
    total += jnp.dot(inverse_high, high, preferred_element_type=F32)
    out_ref[...] = total * (1.0 / ROWS**0.5)


def project(bits, inverse, sources):
    counts = [4, 2, 2, 4, 2, 2]
    specs, begin = [], 0
    for count in counts:
        specs.append(
            pl.BlockSpec(
                (1, 4, PIECE, 128),
                lambda s, bits, begin=begin, count=count: (jnp.clip(s - begin, 0, count - 1), 0, 0, 0),
            )
        )
        begin += count
    return pl.pallas_call(
        project_kernel,
        grid_spec=pltpu.PrefetchScalarGridSpec(
            num_scalar_prefetch=1,
            grid=(16,),
            in_specs=[pl.BlockSpec((K, K), lambda s, bits: (0, 0)), *specs],
            out_specs=pl.BlockSpec(
                (K, 256), lambda s, bits: (0, (bits[0] ^ (s // 8)) * 8 + ((s % 8) ^ bits[1]))
            ),
            scratch_shapes=[pltpu.VMEM((K, 256), F32)],
        ),
        out_shape=jax.ShapeDtypeStruct((K, D), F32),
        compiler_params=PARAMS,
        cost_estimate=pl.CostEstimate(
            flops=3 * 2 * K * K * D, bytes_accessed=9_000_000, transcendentals=0
        ),
        name="project",
    )(bits, inverse, *sources)


def shards(corpus, sketch):
    bits = own_bits()
    sampled, high, low, gram = sketch_rows(corpus, sketch)

    away = correlate(bits, corpus, high, low, gram, 1)
    received = shift(away, core=1)
    kept = correlate(bits, corpus, high, low, gram, 0)
    shape = (2, 2, 2, 4, PIECE, 128)
    received, kept = received.reshape(shape), kept.reshape(shape)
    with jax.named_scope("scatter_x"):
        ahead = shift(kept[1, 0] + received[1, 0], x=1)
        back = shift(kept[1, 1] + received[1, 1], x=-1)
        sum_ahead = kept[0, 0] + received[0, 0]
        sum_back = kept[0, 1] + received[0, 1]
        from_ahead, from_back = sum_ahead + ahead, sum_back + back
    with jax.named_scope("scatter_y"):
        ahead = shift(from_back[0], y=1)
        back = shift(from_back[1], y=-1)
        near, far = from_ahead[0] + ahead, from_ahead[1] + back
    with jax.named_scope("scatter_z"):
        ahead = shift(far[0:2], z=1)
        back = shift(far[2:4], z=-1)
        own, one, two, three = leave_parts(bits, near, ahead, back)
    with jax.named_scope("scatter_upper"):
        one, two, three = shift(one, y=2), shift(two, x=2), shift(three, x=2, y=2)
        own = (own + one) + (two + three)
    with jax.named_scope("total_z"):
        four = shift(own, z=4)
        two, six = shift(own, z=2), shift(own, z=6)
        own = (own + four) + (two + six)

    with jax.named_scope("gather_upper"):
        parts = (own, shift(own, y=2), shift(own, x=2), shift(own, x=2, y=2))
        whole = join_parts(bits, parts)
    with jax.named_scope("gather_z"):
        other = jnp.concatenate([shift(whole[0:2], z=1), shift(whole[2:4], z=-1)])
    with jax.named_scope("gather_y"):
        ahead, back = shift(whole, y=1), shift(other, y=-1)
        quarter = jnp.stack([whole, other, ahead, back])
    with jax.named_scope("gather_x"):
        gram_near = quarter[:, :, 128:, :]
        gram_far = shift(gram_near, x=1)
        ahead, back = shift(quarter[0:2], x=1), shift(quarter[2:4], x=-1)
        gram_other = shift(jnp.concatenate([gram_near, gram_far]), core=1)
        core_quarter = shift(quarter, core=1)
    with jax.named_scope("gather_core"):
        core_ahead, core_back = shift(ahead, core=1), shift(back, core=1)

    inverse = inverse_factor(bits, gram_near, gram_far, gram_other)
    basis = basis_rows(sampled, inverse)
    projected = project(
        bits, inverse, (quarter, ahead, back, core_quarter, core_ahead, core_back)
    )
    return (basis, projected)


def solution(mesh):
    return jax.shard_map(
        shards,
        mesh=mesh,
        in_specs=(P(AXES, None), P()),
        out_specs=(P(AXES, None), P()),
        check_vma=False,
    )
```

```python
import functools

import jax
import jax.numpy as jnp
from jax import lax
from jax.experimental import pallas as pl
from jax.experimental.pallas import tpu as pltpu
from jax.sharding import PartitionSpec as P

AXES = ("rowa", "rowb")
D = 4096
K = 256
ROWS_DEV = 768
ROWS = 196608
NX, NY, NZ = 4, 4, 8
F32 = jnp.float32
BF16 = jnp.bfloat16
PART = 144
KEEP, SEND = 512, 640
PARAMS = pltpu.CompilerParams(vmem_limit_bytes=24 * 1024 * 1024)


def index_of(x, y, z, core):
    return ((x % 2) * 16 + z * 2 + core) * 8 + (x // 2) * 4 + y


def shift(value, x=0, y=0, z=0, core=0):
    pairs = [
        (index_of(i, j, k, c), index_of((i + x) % NX, (j + y) % NY, (k + z) % NZ, (c + core) % 2))
        for i in range(NX)
        for j in range(NY)
        for k in range(NZ)
        for c in range(2)
    ]
    return lax.ppermute(value, AXES, pairs)


def exchange(value):
    groups = [
        [index_of((2 * u + j % 2 - s) % NX, j, 2 * k + p, c) for p in range(2) for j in range(NY) for u in range(2)]
        for s in range(2)
        for k in range(NZ // 2)
        for c in range(2)
    ]
    return lax.all_to_all(value, AXES, 0, 0, axis_index_groups=groups, tiled=True)


def own_bits():
    a, b = lax.axis_index("rowa"), lax.axis_index("rowb")
    return jnp.stack([a % 2, (a // 16 + b) % 2, (a // 2) % 2]).astype(jnp.int32)


def split(value):
    high = value.astype(BF16)
    return high, (value - high.astype(F32)).astype(BF16)


CHUNKS = 4


def sketch_kernel(corpus_ref, sketch_ref, rows_ref, sampled_ref, both_ref, gram_ref, sems):
    chunk = D // CHUNKS
    copies = []
    for k in range(CHUNKS):
        span = pl.ds(k * chunk, chunk)
        copies.append(pltpu.make_async_copy(corpus_ref.at[:, span], rows_ref.at[:, span], sems.at[k]))
    for copy in copies:
        copy.start()
    for k, copy in enumerate(copies):
        copy.wait()
        span = slice(k * chunk, (k + 1) * chunk)
        part = jnp.dot(rows_ref[:, span], sketch_ref[span, :], preferred_element_type=F32)
        sampled_ref[...] = part if k == 0 else sampled_ref[...] + part
    total = None
    for k in range(ROWS_DEV // K):
        block = sampled_ref[k * K : (k + 1) * K, :]
        turned = block.T
        high, low = split(turned)
        both_ref[0:K, k * K : (k + 1) * K] = high
        both_ref[K:, k * K : (k + 1) * K] = low
        part = jnp.dot(turned, block, precision=lax.Precision.HIGHEST, preferred_element_type=F32)
        total = part if k == 0 else total + part
    gram_ref[...] = total


def sketch_rows(corpus, sketch):
    return pl.pallas_call(
        sketch_kernel,
        in_specs=[pl.BlockSpec(memory_space=pl.ANY), pl.BlockSpec(memory_space=pltpu.VMEM)],
        out_specs=[pl.BlockSpec(memory_space=pltpu.VMEM)] * 4,
        out_shape=[
            jax.ShapeDtypeStruct((ROWS_DEV, D), BF16),
            jax.ShapeDtypeStruct((ROWS_DEV, K), F32),
            jax.ShapeDtypeStruct((2 * K, ROWS_DEV), BF16),
            jax.ShapeDtypeStruct((K, K), F32),
        ],
        scratch_shapes=[pltpu.SemaphoreType.DMA((CHUNKS,))],
        compiler_params=pltpu.CompilerParams(vmem_limit_bytes=40 * 1024 * 1024),
        cost_estimate=pl.CostEstimate(
            flops=3 * ROWS_DEV * D * K, bytes_accessed=9_000_000, transcendentals=0
        ),
        name="sketch_rows",
    )(corpus, sketch)


def correlate_kernel(flip, leaves, bits_ref, corpus_ref, both_ref, gram_ref, out_ref):
    core = bits_ref[0] ^ flip
    start = core * 2048 + (bits_ref[1] ^ leaves) * 1024
    size = SEND if leaves else KEEP
    for i in range(4):
        columns = pl.ds(pl.multiple_of(start + 256 * i, 256), 256)
        part = jnp.dot(both_ref[...], corpus_ref[:, columns], preferred_element_type=F32)
        part = part[0:K] + part[K:]
        for q in range(4):
            row = size * i + 128 * q
            out_ref[row : row + 64, :] = part[64 * q : 64 * q + 64, 0:128]
            out_ref[row + 64 : row + 128, :] = part[64 * q : 64 * q + 64, 128:256]
        if leaves:
            lanes = pl.ds(pl.multiple_of(core * 128, 128), 128)
            out_ref[size * i + 512 : size * i + 640, :] = gram_ref[128 * (i // 2) : 128 * (i // 2) + 128, lanes]


def correlate(bits, corpus, both, gram, flip, leaves):
    return pl.pallas_call(
        functools.partial(correlate_kernel, flip, leaves),
        grid_spec=pltpu.PrefetchScalarGridSpec(
            num_scalar_prefetch=1,
            grid=(),
            in_specs=[pl.BlockSpec(memory_space=pltpu.VMEM)] * 3,
            out_specs=pl.BlockSpec(memory_space=pltpu.VMEM),
        ),
        out_shape=jax.ShapeDtypeStruct((4 * (SEND if leaves else KEEP), 128), F32),
        compiler_params=PARAMS,
        cost_estimate=pl.CostEstimate(
            flops=ROWS_DEV * D * K, bytes_accessed=3_000_000, transcendentals=0
        ),
        name=f"correlate{flip}{leaves}",
    )(bits, corpus, both, gram)


def merge_kernel(bits_ref, kept_ref, received_ref, gram_ref, gram_received_ref, *refs):
    out_ref = refs[4]
    even = bits_ref[1] == 0
    for m in range(16):
        d, q = m // 4, m % 4
        rows = slice(128 * m, 128 * m + 128)
        out_ref[m, 0:128, :] = kept_ref[rows, :] + received_ref[rows, :] + refs[d][128 * q : 128 * q + 128, :]
        way = 2 * (m // 8)
        row = 512 + 16 * (m % 8)
        own = slice(SEND * way + row, SEND * way + row + 16)
        other = jnp.where(even, refs[way][row : row + 16, :], refs[way + 1][row : row + 16, :])
        out_ref[m, 128:144, :] = (gram_ref[own, :] + gram_received_ref[own, :]) + other


def merge(bits, kept, received, gram, gram_received, sent):
    return pl.pallas_call(
        merge_kernel,
        grid_spec=pltpu.PrefetchScalarGridSpec(
            num_scalar_prefetch=1,
            grid=(),
            in_specs=[pl.BlockSpec(memory_space=pltpu.VMEM)] * 8,
            out_specs=pl.BlockSpec(memory_space=pltpu.VMEM),
        ),
        out_shape=jax.ShapeDtypeStruct((16, PART, 128), F32),
        compiler_params=PARAMS,
        name="merge",
    )(bits, kept, received, gram, gram_received, *sent)


def total_kernel(bits_ref, parts_ref, out_ref):
    order = [8 * p + 2 * ((j - 1) % 4) + (u ^ (j % 2)) for p in range(2) for j in range(4) for u in range(2)]
    out_ref[...] = functools.reduce(jnp.add, [parts_ref[m] for m in range(16)])

    @pl.when(bits_ref[1] * bits_ref[2] == 1)
    def _():
        out_ref[128:144, :] = functools.reduce(jnp.add, [parts_ref[m, 128:144, :] for m in order])


def total(bits, parts):
    return pl.pallas_call(
        total_kernel,
        grid_spec=pltpu.PrefetchScalarGridSpec(
            num_scalar_prefetch=1,
            grid=(),
            in_specs=[pl.BlockSpec(memory_space=pltpu.VMEM)],
            out_specs=pl.BlockSpec(memory_space=pltpu.VMEM),
        ),
        out_shape=jax.ShapeDtypeStruct((PART, 128), F32),
        compiler_params=PARAMS,
        name="total",
    )(bits, parts)


def eliminate(panel, start):
    count = panel.shape[0] // 8
    lanes = lax.broadcasted_iota(jnp.int32, (8, K), 1)
    below = lax.broadcasted_iota(jnp.int32, (8, K), 0)
    row_of = lax.broadcasted_iota(jnp.int32, (8, 128), 0)
    tiles = [panel[8 * t : 8 * t + 8, :] for t in range(count)]
    for b in range(count):
        first = start + 8 * b
        columns = [
            [jnp.broadcast_to(tiles[t][:, first + k : first + k + 1], (8, 128)) for t in range(b, count)]
            for k in range(8)
        ]
        own = jnp.logical_and(lanes >= first, lanes < first + 8)
        for t in range(b, count):
            fresh = jnp.where(lanes - first == below, 1.0, 0.0) if t == b else 0.0
            tiles[t] = jnp.where(own, fresh, tiles[t])
        pivots = jnp.ones((8, 128), F32)
        for j in range(8):
            lead = columns[j][0]
            pivot = jnp.broadcast_to(lead[j : j + 1, :], (8, 128))
            pivots = jnp.where(row_of == j, pivot, pivots)
            inverse = 1.0 / pivot
            row = tiles[b][j : j + 1, :]
            across = [jnp.broadcast_to(lead[k : k + 1, :], (8, 128)) for k in range(8)]
            for t in range(b, count):
                factor = columns[j][t - b] * inverse
                if t == b:
                    factor = jnp.where(row_of > j, factor, 0.0)
                for k in range(j + 1, 8):
                    columns[k][t - b] = columns[k][t - b] - factor * across[k]
                tiles[t] = tiles[t] - jnp.concatenate([factor, factor], axis=1) * row
        scale = lax.rsqrt(pivots)
        tiles[b] = tiles[b] * jnp.concatenate([scale, scale], axis=1)
    return jnp.concatenate(tiles, axis=0)


def factor_kernel(bits_ref, own_ref, other_ref, out_ref, half_ref, work_ref):
    for m in range(16):
        half_ref[bits_ref[0], 16 * m : 16 * m + 16, :] = own_ref[m]
        half_ref[1 - bits_ref[0], 16 * m : 16 * m + 16, :] = other_ref[m]
    work_ref[:, 0:128] = half_ref[0] / ROWS
    work_ref[:, 128:256] = half_ref[1] / ROWS
    step = 32
    lanes = lax.broadcasted_iota(jnp.int32, (1, K), 1)
    rows = lax.broadcasted_iota(jnp.int32, (step, 1), 0)
    for start in range(0, K, step):
        panel = eliminate(work_ref[start : start + step, :], start)
        end = start + step
        out_ref[start:end, :] = jnp.where(lanes <= rows + start, panel, 0.0)
        own = jnp.logical_and(lanes >= start, lanes < end)
        masked = jnp.where(jnp.logical_and(own, lanes - start > rows), 0.0, panel)
        for a, b in ((end, min(end + step, K)), (min(end + step, K), K)):
            if a < b:
                update = lax.dot_general(
                    panel[:, a:b],
                    masked,
                    (((0,), (0,)), ((), ())),
                    precision=lax.Precision.HIGHEST,
                    preferred_element_type=F32,
                )
                work_ref[a:b, :] = jnp.where(own, 0.0, work_ref[a:b, :]) - update


def inverse_factor(bits, own, other):
    return pl.pallas_call(
        factor_kernel,
        grid_spec=pltpu.PrefetchScalarGridSpec(
            num_scalar_prefetch=1,
            grid=(),
            in_specs=[pl.BlockSpec(memory_space=pltpu.VMEM)] * 2,
            out_specs=pl.BlockSpec(memory_space=pltpu.VMEM),
            scratch_shapes=[pltpu.VMEM((2, K, 128), F32), pltpu.VMEM((K, K), F32)],
        ),
        out_shape=jax.ShapeDtypeStruct((K, K), F32),
        compiler_params=PARAMS,
        cost_estimate=pl.CostEstimate(
            flops=10_000_000_000, bytes_accessed=1_000_000, transcendentals=0
        ),
        name="inverse_factor",
    )(bits, own, other)


def project_columns(bits_ref, flip, inverse_ref, sources, out_ref, work_ref, sems):
    inverse_high, inverse_low = split(inverse_ref[...])
    both = jnp.concatenate([inverse_high, inverse_low], axis=0)
    pieces = [(source, m) for source in sources for m in range(0, source.shape[0], 4)]
    copies = []
    for i, (source, first) in enumerate(pieces):
        rows = [
            jnp.concatenate([source[first + q, 0:64, :], source[first + q, 64:128, :]], axis=1) for q in range(4)
        ]
        high, low = split(jnp.concatenate(rows, axis=0))
        part = jnp.dot(both, high, preferred_element_type=F32)
        part = jnp.dot(inverse_high, low, preferred_element_type=F32) + part[K:] + part[0:K]
        work_ref[i] = part * (1.0 / ROWS**0.5)
        column = (bits_ref[0] ^ (i // 4)) * 2048 + (bits_ref[1] ^ flip) * 1024 + 256 * (i % 4)
        columns = pl.ds(pl.multiple_of(column, 256), 256)
        copies.append(pltpu.make_async_copy(work_ref.at[i], out_ref.at[:, columns], sems.at[i]))
        copies[-1].start()
    return copies


def project_kernel(bits_ref, inverse_ref, sampled_ref, *refs):
    sources, (out_ref, basis_ref, work_ref, rows_ref, sems) = refs[:-5], refs[-5:]
    rows_ref[...] = lax.dot_general(
        sampled_ref[...],
        inverse_ref[...],
        (((1,), (1,)), ((), ())),
        precision=lax.Precision.HIGHEST,
        preferred_element_type=F32,
    )
    copy = pltpu.make_async_copy(rows_ref, basis_ref, sems.at[8])
    copy.start()
    for other in project_columns(bits_ref, 0, inverse_ref, sources, out_ref, work_ref, sems):
        other.wait()
    copy.wait()


def project_rest_kernel(bits_ref, inverse_ref, *refs):
    sources, (out_ref, work_ref, sems) = refs[:-4], refs[-3:]
    for copy in project_columns(bits_ref, 1, inverse_ref, sources, out_ref, work_ref, sems):
        copy.wait()


def project(bits, inverse, sources, sampled=None, into=None):
    whole = pl.BlockSpec(memory_space=pltpu.VMEM)
    away = pl.BlockSpec(memory_space=pl.ANY)
    out_shape = [jax.ShapeDtypeStruct((K, D), F32)]
    scratch = [pltpu.VMEM((8, K, 256), F32)]
    if into is None:
        kernel = project_kernel
        operands, in_specs = [inverse, sampled, *sources], [whole] * (2 + len(sources))
        out_shape.append(jax.ShapeDtypeStruct((ROWS_DEV, K), F32))
        scratch.append(pltpu.VMEM((ROWS_DEV, K), F32))
    else:
        kernel = project_rest_kernel
        operands, in_specs = [inverse, *sources, into], [whole] * (1 + len(sources)) + [away]
    return pl.pallas_call(
        kernel,
        grid_spec=pltpu.PrefetchScalarGridSpec(
            num_scalar_prefetch=1,
            grid=(),
            in_specs=in_specs,
            out_specs=[away] * len(out_shape),
            scratch_shapes=scratch + [pltpu.SemaphoreType.DMA((9,))],
        ),
        out_shape=out_shape,
        input_output_aliases={} if into is None else {len(operands): 0},
        compiler_params=PARAMS,
        cost_estimate=pl.CostEstimate(
            flops=3 * K * K * D, bytes_accessed=5_000_000, transcendentals=0
        ),
        name="project" if into is None else "project_rest",
    )(bits, *operands)


WAYS = ({"x": 1}, {"x": -1}, {"y": 1}, {"y": -1})


def shards(corpus, sketch):
    bits = own_bits()
    corpus, sampled, both, gram = sketch_rows(corpus, sketch)

    made = functools.partial(correlate, bits, corpus, both, gram)
    far_received = shift(made(1, 1), core=1)
    near_received = shift(made(1, 0), core=1)
    far, near = made(0, 1), made(0, 0)
    with jax.named_scope("scatter_neighbours"):
        rows = [slice(SEND * d, SEND * d + SEND) for d in range(4)]
        sent = [shift(far[rows[d]] + far_received[rows[d]], **WAYS[d]) for d in range(4)]
        parts = merge(bits, near, near_received, far, far_received, sent)
    with jax.named_scope("scatter_rest"):
        own = total(bits, exchange(parts))
    with jax.named_scope("total_z"):
        four = shift(own, z=4)
        two, six = shift(own, z=2), shift(own, z=6)
        own = (own + four) + (two + six)

    with jax.named_scope("gather_rest"):
        near = exchange(jnp.broadcast_to(own[None], (16, PART, 128)))
    with jax.named_scope("gather_gram"):
        gram_own = near[:, 128:, :]
        gram_other = shift(gram_own, core=1)
    with jax.named_scope("gather_neighbours"):
        far = [shift(near[4 * d : 4 * d + 4], **WAYS[d]) for d in range(4)]
    near_late, gram_other = lax.optimization_barrier((near, gram_other))
    with jax.named_scope("gather_core"):
        near_other = shift(near_late, core=1)
    inverse = inverse_factor(bits, gram_own, gram_other)
    *far, inverse = lax.optimization_barrier((*far, inverse))
    with jax.named_scope("gather_core"):
        far_other = [shift(part, core=1) for part in far]

    half, basis = project(bits, inverse, (near, near_other), sampled=sampled)
    (projected,) = project(bits, inverse, (*far, *far_other), into=half)
    return (basis, projected)


def solution(mesh):
    return jax.shard_map(
        shards,
        mesh=mesh,
        in_specs=(P(AXES, None), P()),
        out_specs=(P(AXES, None), P()),
        check_vma=False,
    )
```

```python
import functools

import jax
import jax.numpy as jnp
from jax import lax
from jax.experimental import pallas as pl
from jax.experimental.pallas import tpu as pltpu
from jax.sharding import PartitionSpec as P

AXES = ("rowa", "rowb")
D = 4096
K = 256
ROWS_DEV = 768
ROWS = 196608
NX, NY, NZ = 4, 4, 8
F32 = jnp.float32
BF16 = jnp.bfloat16
PART = 160
KEEP, SEND = 512, 640
PARAMS = pltpu.CompilerParams(vmem_limit_bytes=24 * 1024 * 1024)


def index_of(x, y, z, core):
    return ((x % 2) * 16 + z * 2 + core) * 8 + (x // 2) * 4 + y


def shift(value, x=0, y=0, z=0, core=0):
    pairs = [
        (index_of(i, j, k, c), index_of((i + x) % NX, (j + y) % NY, (k + z) % NZ, (c + core) % 2))
        for i in range(NX)
        for j in range(NY)
        for k in range(NZ)
        for c in range(2)
    ]
    return lax.ppermute(value, AXES, pairs)


def exchange(value, planes):
    groups = [
        [
            index_of((2 * u + j % 2 - s) % NX, j, planes * k + p, c)
            for p in range(planes)
            for j in range(NY)
            for u in range(2)
        ]
        for s in range(2)
        for k in range(NZ // planes)
        for c in range(2)
    ]
    return lax.all_to_all(value, AXES, 0, 0, axis_index_groups=groups, tiled=True)


def own_bits():
    a, b = lax.axis_index("rowa"), lax.axis_index("rowb")
    return jnp.stack([a % 2, (a // 16 + b) % 2, (b // 2) % 2, (a // 2) % 2]).astype(jnp.int32)


def split(value):
    high = value.astype(BF16)
    return high, (value - high.astype(F32)).astype(BF16)


CHUNKS = 4


def sketch_kernel(corpus_ref, sketch_ref, rows_ref, sampled_ref, both_ref, gram_ref, sems):
    chunk = D // CHUNKS
    copies = []
    for k in range(CHUNKS):
        span = pl.ds(k * chunk, chunk)
        copies.append(pltpu.make_async_copy(corpus_ref.at[:, span], rows_ref.at[:, span], sems.at[k]))
    for copy in copies:
        copy.start()
    for k, copy in enumerate(copies):
        copy.wait()
        span = slice(k * chunk, (k + 1) * chunk)
        part = jnp.dot(rows_ref[:, span], sketch_ref[span, :], preferred_element_type=F32)
        sampled_ref[...] = part if k == 0 else sampled_ref[...] + part
    total = None
    for k in range(ROWS_DEV // K):
        block = sampled_ref[k * K : (k + 1) * K, :]
        turned = block.T
        high, low = split(turned)
        both_ref[0:K, k * K : (k + 1) * K] = high
        both_ref[K:, k * K : (k + 1) * K] = low
        part = jnp.dot(turned, block, precision=lax.Precision.HIGHEST, preferred_element_type=F32)
        total = part if k == 0 else total + part
    gram_ref[...] = total


def sketch_rows(corpus, sketch):
    return pl.pallas_call(
        sketch_kernel,
        in_specs=[pl.BlockSpec(memory_space=pl.ANY), pl.BlockSpec(memory_space=pltpu.VMEM)],
        out_specs=[pl.BlockSpec(memory_space=pltpu.VMEM)] * 4,
        out_shape=[
            jax.ShapeDtypeStruct((ROWS_DEV, D), BF16),
            jax.ShapeDtypeStruct((ROWS_DEV, K), F32),
            jax.ShapeDtypeStruct((2 * K, ROWS_DEV), BF16),
            jax.ShapeDtypeStruct((K, K), F32),
        ],
        scratch_shapes=[pltpu.SemaphoreType.DMA((CHUNKS,))],
        compiler_params=pltpu.CompilerParams(vmem_limit_bytes=40 * 1024 * 1024),
        cost_estimate=pl.CostEstimate(
            flops=3 * ROWS_DEV * D * K, bytes_accessed=9_000_000, transcendentals=0
        ),
        name="sketch_rows",
    )(corpus, sketch)


def correlate_kernel(flip, leaves, bits_ref, corpus_ref, both_ref, gram_ref, out_ref):
    core = bits_ref[0] ^ flip
    start = core * 2048 + (bits_ref[1] ^ leaves) * 1024
    size = SEND if leaves else KEEP
    for i in range(4):
        columns = pl.ds(pl.multiple_of(start + 256 * i, 256), 256)
        part = jnp.dot(both_ref[...], corpus_ref[:, columns], preferred_element_type=F32)
        part = part[0:K] + part[K:]
        for q in range(4):
            row = size * i + 128 * q
            out_ref[row : row + 64, :] = part[64 * q : 64 * q + 64, 0:128]
            out_ref[row + 64 : row + 128, :] = part[64 * q : 64 * q + 64, 128:256]
        if leaves:
            lanes = pl.ds(pl.multiple_of(core * 128, 128), 128)
            out_ref[size * i + 512 : size * i + 640, :] = gram_ref[128 * (i // 2) : 128 * (i // 2) + 128, lanes]


def correlate(bits, corpus, both, gram, flip, leaves):
    return pl.pallas_call(
        functools.partial(correlate_kernel, flip, leaves),
        grid_spec=pltpu.PrefetchScalarGridSpec(
            num_scalar_prefetch=1,
            grid=(),
            in_specs=[pl.BlockSpec(memory_space=pltpu.VMEM)] * 3,
            out_specs=pl.BlockSpec(memory_space=pltpu.VMEM),
        ),
        out_shape=jax.ShapeDtypeStruct((4 * (SEND if leaves else KEEP), 128), F32),
        compiler_params=PARAMS,
        cost_estimate=pl.CostEstimate(
            flops=ROWS_DEV * D * K, bytes_accessed=3_000_000, transcendentals=0
        ),
        name=f"correlate{flip}{leaves}",
    )(bits, corpus, both, gram)


def merge_kernel(bits_ref, kept_ref, received_ref, gram_ref, gram_received_ref, *refs):
    out_ref = refs[4]
    even = bits_ref[1] == 0
    for m in range(16):
        d, q = m // 4, m % 4
        rows = slice(128 * m, 128 * m + 128)
        out_ref[m, 0:128, :] = kept_ref[rows, :] + received_ref[rows, :] + refs[d][128 * q : 128 * q + 128, :]
        way = 2 * (m % 8 // 4)
        row = 512 + 32 * (m % 4)
        own = slice(SEND * way + row, SEND * way + row + 32)
        other = jnp.where(even, refs[way][row : row + 32, :], refs[way + 1][row : row + 32, :])
        out_ref[m, 128:160, :] = (gram_ref[own, :] + gram_received_ref[own, :]) + other


def merge(bits, kept, received, gram, gram_received, sent):
    return pl.pallas_call(
        merge_kernel,
        grid_spec=pltpu.PrefetchScalarGridSpec(
            num_scalar_prefetch=1,
            grid=(),
            in_specs=[pl.BlockSpec(memory_space=pltpu.VMEM)] * 8,
            out_specs=pl.BlockSpec(memory_space=pltpu.VMEM),
        ),
        out_shape=jax.ShapeDtypeStruct((16, PART, 128), F32),
        compiler_params=PARAMS,
        name="merge",
    )(bits, kept, received, gram, gram_received, *sent)


def total_kernel(bits_ref, parts_ref, out_ref):
    order = [8 * p + 2 * ((j - 1) % 4) + (u ^ (j % 2)) for p in range(2) for j in range(4) for u in range(2)]
    out_ref[...] = functools.reduce(jnp.add, [parts_ref[m] for m in range(16)])

    @pl.when(bits_ref[1] * bits_ref[2] == 1)
    def _():
        out_ref[128:160, :] = functools.reduce(jnp.add, [parts_ref[m, 128:160, :] for m in order])


def total(bits, parts):
    return pl.pallas_call(
        total_kernel,
        grid_spec=pltpu.PrefetchScalarGridSpec(
            num_scalar_prefetch=1,
            grid=(),
            in_specs=[pl.BlockSpec(memory_space=pltpu.VMEM)],
            out_specs=pl.BlockSpec(memory_space=pltpu.VMEM),
        ),
        out_shape=jax.ShapeDtypeStruct((PART, 128), F32),
        compiler_params=PARAMS,
        name="total",
    )(bits, parts)


def eliminate(panel, start):
    count = panel.shape[0] // 8
    lanes = lax.broadcasted_iota(jnp.int32, (8, K), 1)
    below = lax.broadcasted_iota(jnp.int32, (8, K), 0)
    row_of = lax.broadcasted_iota(jnp.int32, (8, 128), 0)
    tiles = [panel[8 * t : 8 * t + 8, :] for t in range(count)]
    for b in range(count):
        first = start + 8 * b
        columns = [
            [jnp.broadcast_to(tiles[t][:, first + k : first + k + 1], (8, 128)) for t in range(b, count)]
            for k in range(8)
        ]
        own = jnp.logical_and(lanes >= first, lanes < first + 8)
        for t in range(b, count):
            fresh = jnp.where(lanes - first == below, 1.0, 0.0) if t == b else 0.0
            tiles[t] = jnp.where(own, fresh, tiles[t])
        pivots = jnp.ones((8, 128), F32)
        for j in range(8):
            lead = columns[j][0]
            pivot = jnp.broadcast_to(lead[j : j + 1, :], (8, 128))
            pivots = jnp.where(row_of == j, pivot, pivots)
            inverse = 1.0 / pivot
            row = tiles[b][j : j + 1, :]
            across = [jnp.broadcast_to(lead[k : k + 1, :], (8, 128)) for k in range(8)]
            for t in range(b, count):
                factor = columns[j][t - b] * inverse
                if t == b:
                    factor = jnp.where(row_of > j, factor, 0.0)
                for k in range(j + 1, 8):
                    columns[k][t - b] = columns[k][t - b] - factor * across[k]
                tiles[t] = tiles[t] - jnp.concatenate([factor, factor], axis=1) * row
        scale = lax.rsqrt(pivots)
        tiles[b] = tiles[b] * jnp.concatenate([scale, scale], axis=1)
    return jnp.concatenate(tiles, axis=0)


def factor_kernel(bits_ref, own_ref, other_ref, out_ref, half_ref, work_ref):
    for m in range(8):
        half_ref[bits_ref[0], 32 * m : 32 * m + 32, :] = own_ref[m]
        half_ref[1 - bits_ref[0], 32 * m : 32 * m + 32, :] = other_ref[m]
    work_ref[:, 0:128] = half_ref[0] / ROWS
    work_ref[:, 128:256] = half_ref[1] / ROWS
    step = 32
    lanes = lax.broadcasted_iota(jnp.int32, (1, K), 1)
    rows = lax.broadcasted_iota(jnp.int32, (step, 1), 0)
    for start in range(0, K, step):
        panel = eliminate(work_ref[start : start + step, :], start)
        end = start + step
        out_ref[start:end, :] = jnp.where(lanes <= rows + start, panel, 0.0)
        own = jnp.logical_and(lanes >= start, lanes < end)
        masked = jnp.where(jnp.logical_and(own, lanes - start > rows), 0.0, panel)
        for a, b in ((end, min(end + step, K)), (min(end + step, K), K)):
            if a < b:
                update = lax.dot_general(
                    panel[:, a:b],
                    masked,
                    (((0,), (0,)), ((), ())),
                    precision=lax.Precision.HIGHEST,
                    preferred_element_type=F32,
                )
                work_ref[a:b, :] = jnp.where(own, 0.0, work_ref[a:b, :]) - update


def inverse_factor(bits, own, other):
    return pl.pallas_call(
        factor_kernel,
        grid_spec=pltpu.PrefetchScalarGridSpec(
            num_scalar_prefetch=1,
            grid=(),
            in_specs=[pl.BlockSpec(memory_space=pltpu.VMEM)] * 2,
            out_specs=pl.BlockSpec(memory_space=pltpu.VMEM),
            scratch_shapes=[pltpu.VMEM((2, K, 128), F32), pltpu.VMEM((K, K), F32)],
        ),
        out_shape=jax.ShapeDtypeStruct((K, K), F32),
        compiler_params=PARAMS,
        cost_estimate=pl.CostEstimate(
            flops=10_000_000_000, bytes_accessed=1_000_000, transcendentals=0
        ),
        name="inverse_factor",
    )(bits, own, other)


def project_columns(apart, bits_ref, inverse_ref, sources, out_ref, work_ref, sems):
    inverse_high, inverse_low = split(inverse_ref[...])
    both = jnp.concatenate([inverse_high, inverse_low], axis=0)
    copies = []
    for i in range(2 * len(sources)):
        source, first = sources[i // 2], 4 * (i % 2)
        rows = [
            jnp.concatenate([source[first + q, 0:64, :], source[first + q, 64:128, :]], axis=1) for q in range(4)
        ]
        high, low = split(jnp.concatenate(rows, axis=0))
        part = jnp.dot(both, high, preferred_element_type=F32)
        part = jnp.dot(inverse_high, low, preferred_element_type=F32) + part[K:] + part[0:K]
        work_ref[i] = part * (1.0 / ROWS**0.5)
        core, plane, level = apart[i // 2]
        column = (bits_ref[0] ^ core) * 2048 + (bits_ref[1] ^ plane) * 1024 + (bits_ref[3] ^ level) * 512
        columns = pl.ds(pl.multiple_of(column + 256 * (i % 2), 256), 256)
        copies.append(pltpu.make_async_copy(work_ref.at[i], out_ref.at[:, columns], sems.at[i]))
        copies[-1].start()
    return copies


def project_kernel(apart, bits_ref, inverse_ref, *refs):
    out_ref, work_ref, sems = refs[-3:]
    for copy in project_columns(apart, bits_ref, inverse_ref, refs[: len(apart)], out_ref, work_ref, sems):
        copy.wait()


def basis_kernel(apart, bits_ref, inverse_ref, *refs):
    sampled_ref = refs[len(apart)]
    out_ref, basis_ref, work_ref, rows_ref, sems = refs[-5:]
    copies = project_columns(apart, bits_ref, inverse_ref, refs[: len(apart)], out_ref, work_ref, sems)
    rows_ref[...] = lax.dot_general(
        sampled_ref[...],
        inverse_ref[...],
        (((1,), (1,)), ((), ())),
        precision=lax.Precision.HIGHEST,
        preferred_element_type=F32,
    )
    last = pltpu.make_async_copy(rows_ref, basis_ref, sems.at[2 * len(apart)])
    last.start()
    for copy in copies:
        copy.wait()
    last.wait()


def project(bits, inverse, sources, apart, sampled=None, into=None):
    whole = pl.BlockSpec(memory_space=pltpu.VMEM)
    away = pl.BlockSpec(memory_space=pl.ANY)
    operands, in_specs = [inverse, *sources], [whole] * (1 + len(sources))
    out_shape = [jax.ShapeDtypeStruct((K, D), F32)]
    scratch = [pltpu.VMEM((2 * len(sources), K, 256), F32)]
    if sampled is not None:
        operands.append(sampled)
        in_specs.append(whole)
        out_shape.append(jax.ShapeDtypeStruct((ROWS_DEV, K), F32))
        scratch.append(pltpu.VMEM((ROWS_DEV, K), F32))
    if into is not None:
        operands.append(into)
        in_specs.append(away)
    kernel = project_kernel if sampled is None else basis_kernel
    return pl.pallas_call(
        functools.partial(kernel, apart),
        grid_spec=pltpu.PrefetchScalarGridSpec(
            num_scalar_prefetch=1,
            grid=(),
            in_specs=in_specs,
            out_specs=[away] * len(out_shape),
            scratch_shapes=scratch + [pltpu.SemaphoreType.DMA((2 * len(sources) + 1,))],
        ),
        out_shape=out_shape,
        input_output_aliases={} if into is None else {len(operands): 0},
        compiler_params=PARAMS,
        cost_estimate=pl.CostEstimate(
            flops=6 * K * K * 512 * len(sources), bytes_accessed=4_000_000, transcendentals=0
        ),
        name=f"project{len(sources)}",
    )(bits, *operands)


WAYS = ({"x": 1}, {"x": -1}, {"y": 1}, {"y": -1})


def shards(corpus, sketch):
    bits = own_bits()
    corpus, sampled, both, gram = sketch_rows(corpus, sketch)

    made = functools.partial(correlate, bits, corpus, both, gram)
    far_received = shift(made(1, 1), core=1)
    near_received = shift(made(1, 0), core=1)
    far, near = made(0, 1), made(0, 0)
    with jax.named_scope("scatter_neighbours"):
        rows = [slice(SEND * d, SEND * d + SEND) for d in range(4)]
        sent = [shift(far[rows[d]] + far_received[rows[d]], **WAYS[d]) for d in range(4)]
        parts = merge(bits, near, near_received, far, far_received, sent)
    with jax.named_scope("scatter_rest"):
        own = total(bits, exchange(parts, 2))
    with jax.named_scope("total_z"):
        four = shift(own, z=4)
        two, six = shift(own, z=2), shift(own, z=6)
        own = (own + four) + (two + six)

    with jax.named_scope("gather_rest"):
        near = exchange(jnp.broadcast_to(own[None], (8, PART, 128)), 1)
    with jax.named_scope("gather_gram"):
        gram_own = near[:, 128:, :]
        gram_other = shift(gram_own, core=1)
    with jax.named_scope("gather_neighbours"):
        rows = near[:, 0:128, :]
        far = [shift(rows, y=1, z=-1), shift(rows, x=1), shift(rows, z=1)]
    near_late, gram_other = lax.optimization_barrier((near, gram_other))
    with jax.named_scope("gather_core"):
        near_other = shift(near_late, core=1)
    inverse = inverse_factor(bits, gram_own, gram_other)
    quarters = ((1, 1), (1, 0), (0, 1))
    projected, basis = project(
        bits, inverse, (near, near_other), ((0, 0, 0), (1, 0, 0)), sampled=sampled
    )
    *far, projected = lax.optimization_barrier((*far, projected))
    with jax.named_scope("gather_core"):
        far_other = [shift(part, core=1) for part in far]
    (projected,) = project(bits, inverse, far, tuple((0, *q) for q in quarters), into=projected)
    (projected,) = project(bits, inverse, far_other, tuple((1, *q) for q in quarters), into=projected)
    return (basis, projected)


def solution(mesh):
    return jax.shard_map(
        shards,
        mesh=mesh,
        in_specs=(P(AXES, None), P()),
        out_specs=(P(AXES, None), P()),
        check_vma=False,
    )
```

```python
import functools

import jax
import jax.numpy as jnp
from jax import lax
from jax.experimental import pallas as pl
from jax.experimental.pallas import tpu as pltpu
from jax.sharding import PartitionSpec as P

AXES = ("rowa", "rowb")
D = 4096
K = 256
ROWS_DEV = 768
ROWS = 196608
NX, NY, NZ = 4, 4, 8
F32 = jnp.float32
BF16 = jnp.bfloat16
PART = 160
KEEP, SEND = 512, 640
PARAMS = pltpu.CompilerParams(vmem_limit_bytes=24 * 1024 * 1024)


def index_of(x, y, z, core):
    return ((x % 2) * 16 + z * 2 + core) * 8 + (x // 2) * 4 + y


def shift(value, x=0, y=0, z=0, core=0):
    pairs = [
        (index_of(i, j, k, c), index_of((i + x) % NX, (j + y) % NY, (k + z) % NZ, (c + core) % 2))
        for i in range(NX)
        for j in range(NY)
        for k in range(NZ)
        for c in range(2)
    ]
    return lax.ppermute(value, AXES, pairs)


def exchange(value, planes):
    groups = [
        [
            index_of((2 * u + j % 2 - s) % NX, j, planes * k + p, c)
            for p in range(planes)
            for j in range(NY)
            for u in range(2)
        ]
        for s in range(2)
        for k in range(NZ // planes)
        for c in range(2)
    ]
    return lax.all_to_all(value, AXES, 0, 0, axis_index_groups=groups, tiled=True)


def own_bits():
    a, b = lax.axis_index("rowa"), lax.axis_index("rowb")
    return jnp.stack([a % 2, (a // 16 + b) % 2, (b // 2) % 2, (a // 2) % 2]).astype(jnp.int32)


def split(value):
    high = value.astype(BF16)
    return high, (value - high.astype(F32)).astype(BF16)


CHUNKS = 4


def sketch_kernel(bits_ref, corpus_ref, sketch_ref, rows_ref, sampled_ref, both_ref, gram_ref, away_ref, sems):
    chunk = D // CHUNKS
    copies = []
    for k in range(CHUNKS):
        span = pl.ds(k * chunk, chunk)
        copies.append(pltpu.make_async_copy(corpus_ref.at[:, span], rows_ref.at[:, span], sems.at[k]))
    for copy in copies:
        copy.start()
    for k, copy in enumerate(copies):
        copy.wait()
        span = slice(k * chunk, (k + 1) * chunk)
        part = jnp.dot(rows_ref[:, span], sketch_ref[span, :], preferred_element_type=F32)
        sampled_ref[...] = part if k == 0 else sampled_ref[...] + part
    total = None
    for k in range(ROWS_DEV // K):
        block = sampled_ref[k * K : (k + 1) * K, :]
        turned = block.T
        high, low = split(turned)
        both_ref[0:K, k * K : (k + 1) * K] = high
        both_ref[K:, k * K : (k + 1) * K] = low
        part = jnp.dot(turned, block, precision=lax.Precision.HIGHEST, preferred_element_type=F32)
        total = part if k == 0 else total + part
    gram_ref[...] = total
    correlate_kernel(1, 1, bits_ref, rows_ref, both_ref, gram_ref, away_ref)


def sketch_rows(bits, corpus, sketch):
    return pl.pallas_call(
        sketch_kernel,
        grid_spec=pltpu.PrefetchScalarGridSpec(
            num_scalar_prefetch=1,
            grid=(),
            in_specs=[pl.BlockSpec(memory_space=pl.ANY), pl.BlockSpec(memory_space=pltpu.VMEM)],
            out_specs=[pl.BlockSpec(memory_space=pltpu.VMEM)] * 5,
            scratch_shapes=[pltpu.SemaphoreType.DMA((CHUNKS,))],
        ),
        out_shape=[
            jax.ShapeDtypeStruct((ROWS_DEV, D), BF16),
            jax.ShapeDtypeStruct((ROWS_DEV, K), F32),
            jax.ShapeDtypeStruct((2 * K, ROWS_DEV), BF16),
            jax.ShapeDtypeStruct((K, K), F32),
            jax.ShapeDtypeStruct((4 * SEND, 128), F32),
        ],
        compiler_params=pltpu.CompilerParams(vmem_limit_bytes=40 * 1024 * 1024),
        cost_estimate=pl.CostEstimate(
            flops=3 * ROWS_DEV * D * K, bytes_accessed=9_000_000, transcendentals=0
        ),
        name="sketch_rows",
    )(bits, corpus, sketch)


def correlate_kernel(flip, leaves, bits_ref, corpus_ref, both_ref, gram_ref, out_ref):
    core = bits_ref[0] ^ flip
    start = core * 2048 + (bits_ref[1] ^ leaves) * 1024
    size = SEND if leaves else KEEP
    for i in range(4):
        columns = pl.ds(pl.multiple_of(start + 256 * i, 256), 256)
        part = jnp.dot(both_ref[...], corpus_ref[:, columns], preferred_element_type=F32)
        part = part[0:K] + part[K:]
        for q in range(4):
            row = size * i + 128 * q
            out_ref[row : row + 64, :] = part[64 * q : 64 * q + 64, 0:128]
            out_ref[row + 64 : row + 128, :] = part[64 * q : 64 * q + 64, 128:256]
        if leaves:
            lanes = pl.ds(pl.multiple_of(core * 128, 128), 128)
            out_ref[size * i + 512 : size * i + 640, :] = gram_ref[128 * (i // 2) : 128 * (i // 2) + 128, lanes]


def correlate_some_kernel(which, bits_ref, corpus_ref, both_ref, gram_ref, *out_refs):
    for (flip, leaves), out_ref in zip(which, out_refs):
        correlate_kernel(flip, leaves, bits_ref, corpus_ref, both_ref, gram_ref, out_ref)


def correlate(bits, corpus, both, gram, which):
    return pl.pallas_call(
        functools.partial(correlate_some_kernel, which),
        grid_spec=pltpu.PrefetchScalarGridSpec(
            num_scalar_prefetch=1,
            grid=(),
            in_specs=[pl.BlockSpec(memory_space=pltpu.VMEM)] * 3,
            out_specs=[pl.BlockSpec(memory_space=pltpu.VMEM)] * len(which),
        ),
        out_shape=[
            jax.ShapeDtypeStruct((4 * (SEND if leaves else KEEP), 128), F32) for _, leaves in which
        ],
        compiler_params=PARAMS,
        cost_estimate=pl.CostEstimate(
            flops=ROWS_DEV * D * K * len(which), bytes_accessed=3_000_000, transcendentals=0
        ),
        name=f"correlate{len(which)}",
    )(bits, corpus, both, gram)


def merge_kernel(bits_ref, kept_ref, received_ref, gram_ref, gram_received_ref, *refs):
    out_ref = refs[4]
    even = bits_ref[1] == 0
    for m in range(16):
        d, q = m // 4, m % 4
        rows = slice(128 * m, 128 * m + 128)
        out_ref[m, 0:128, :] = kept_ref[rows, :] + received_ref[rows, :] + refs[d][128 * q : 128 * q + 128, :]
        way = 2 * (m % 8 // 4)
        row = 512 + 32 * (m % 4)
        own = slice(SEND * way + row, SEND * way + row + 32)
        other = jnp.where(even, refs[way][row : row + 32, :], refs[way + 1][row : row + 32, :])
        out_ref[m, 128:160, :] = (gram_ref[own, :] + gram_received_ref[own, :]) + other


def merge(bits, kept, received, gram, gram_received, sent):
    return pl.pallas_call(
        merge_kernel,
        grid_spec=pltpu.PrefetchScalarGridSpec(
            num_scalar_prefetch=1,
            grid=(),
            in_specs=[pl.BlockSpec(memory_space=pltpu.VMEM)] * 8,
            out_specs=pl.BlockSpec(memory_space=pltpu.VMEM),
        ),
        out_shape=jax.ShapeDtypeStruct((16, PART, 128), F32),
        compiler_params=PARAMS,
        name="merge",
    )(bits, kept, received, gram, gram_received, *sent)


def total_kernel(bits_ref, parts_ref, out_ref):
    order = [8 * p + 2 * ((j - 1) % 4) + (u ^ (j % 2)) for p in range(2) for j in range(4) for u in range(2)]
    out_ref[...] = functools.reduce(jnp.add, [parts_ref[m] for m in range(16)])

    @pl.when(bits_ref[1] * bits_ref[2] == 1)
    def _():
        out_ref[128:160, :] = functools.reduce(jnp.add, [parts_ref[m, 128:160, :] for m in order])


def total(bits, parts):
    return pl.pallas_call(
        total_kernel,
        grid_spec=pltpu.PrefetchScalarGridSpec(
            num_scalar_prefetch=1,
            grid=(),
            in_specs=[pl.BlockSpec(memory_space=pltpu.VMEM)],
            out_specs=pl.BlockSpec(memory_space=pltpu.VMEM),
        ),
        out_shape=jax.ShapeDtypeStruct((PART, 128), F32),
        compiler_params=PARAMS,
        name="total",
    )(bits, parts)


def eliminate(panel, start):
    count = panel.shape[0] // 8
    lanes = lax.broadcasted_iota(jnp.int32, (8, K), 1)
    below = lax.broadcasted_iota(jnp.int32, (8, K), 0)
    row_of = lax.broadcasted_iota(jnp.int32, (8, 128), 0)
    tiles = [panel[8 * t : 8 * t + 8, :] for t in range(count)]
    for b in range(count):
        first = start + 8 * b
        columns = [
            [jnp.broadcast_to(tiles[t][:, first + k : first + k + 1], (8, 128)) for t in range(b, count)]
            for k in range(8)
        ]
        own = jnp.logical_and(lanes >= first, lanes < first + 8)
        for t in range(b, count):
            fresh = jnp.where(lanes - first == below, 1.0, 0.0) if t == b else 0.0
            tiles[t] = jnp.where(own, fresh, tiles[t])
        pivots = jnp.ones((8, 128), F32)
        for j in range(8):
            lead = columns[j][0]
            pivot = jnp.broadcast_to(lead[j : j + 1, :], (8, 128))
            pivots = jnp.where(row_of == j, pivot, pivots)
            inverse = 1.0 / pivot
            row = tiles[b][j : j + 1, :]
            across = [jnp.broadcast_to(lead[k : k + 1, :], (8, 128)) for k in range(8)]
            for t in range(b, count):
                factor = columns[j][t - b] * inverse
                if t == b:
                    factor = jnp.where(row_of > j, factor, 0.0)
                for k in range(j + 1, 8):
                    columns[k][t - b] = columns[k][t - b] - factor * across[k]
                tiles[t] = tiles[t] - jnp.concatenate([factor, factor], axis=1) * row
        scale = lax.rsqrt(pivots)
        tiles[b] = tiles[b] * jnp.concatenate([scale, scale], axis=1)
    return jnp.concatenate(tiles, axis=0)


def factor_kernel(bits_ref, own_ref, other_ref, out_ref, half_ref, work_ref):
    for m in range(8):
        half_ref[bits_ref[0], 32 * m : 32 * m + 32, :] = own_ref[m]
        half_ref[1 - bits_ref[0], 32 * m : 32 * m + 32, :] = other_ref[m]
    work_ref[:, 0:128] = half_ref[0] / ROWS
    work_ref[:, 128:256] = half_ref[1] / ROWS
    step = 64
    lanes = lax.broadcasted_iota(jnp.int32, (1, K), 1)
    rows = lax.broadcasted_iota(jnp.int32, (step, 1), 0)
    for start in range(0, K, step):
        panel = eliminate(work_ref[start : start + step, :], start)
        end = start + step
        out_ref[start:end, :] = jnp.where(lanes <= rows + start, panel, 0.0)
        own = jnp.logical_and(lanes >= start, lanes < end)
        masked = jnp.where(jnp.logical_and(own, lanes - start > rows), 0.0, panel)
        if end < K:
            update = lax.dot_general(
                panel[:, end:],
                masked,
                (((0,), (0,)), ((), ())),
                precision=lax.Precision.HIGHEST,
                preferred_element_type=F32,
            )
            work_ref[end:, :] = jnp.where(own, 0.0, work_ref[end:, :]) - update


def inverse_factor(bits, own, other):
    return pl.pallas_call(
        factor_kernel,
        grid_spec=pltpu.PrefetchScalarGridSpec(
            num_scalar_prefetch=1,
            grid=(),
            in_specs=[pl.BlockSpec(memory_space=pltpu.VMEM)] * 2,
            out_specs=pl.BlockSpec(memory_space=pltpu.VMEM),
            scratch_shapes=[pltpu.VMEM((2, K, 128), F32), pltpu.VMEM((K, K), F32)],
        ),
        out_shape=jax.ShapeDtypeStruct((K, K), F32),
        compiler_params=PARAMS,
        cost_estimate=pl.CostEstimate(
            flops=10_000_000_000, bytes_accessed=1_000_000, transcendentals=0
        ),
        name="inverse_factor",
    )(bits, own, other)


def project_columns(apart, bits_ref, inverse_ref, sources, out_ref, work_ref, sems):
    inverse_high, inverse_low = split(inverse_ref[...])
    both = jnp.concatenate([inverse_high, inverse_low], axis=0)
    copies = []
    for i, source in enumerate(sources):
        rows = [
            jnp.concatenate([source[4 * h + q, a : a + 64, :] for h in range(2) for a in (0, 64)], axis=1)
            for q in range(4)
        ]
        high, low = split(jnp.concatenate(rows, axis=0))
        part = jnp.dot(both, high, preferred_element_type=F32)
        part = jnp.dot(inverse_high, low, preferred_element_type=F32) + part[K:] + part[0:K]
        work_ref[i] = part * (1.0 / ROWS**0.5)
        core, plane, level = apart[i]
        column = (bits_ref[0] ^ core) * 2048 + (bits_ref[1] ^ plane) * 1024 + (bits_ref[3] ^ level) * 512
        columns = pl.ds(pl.multiple_of(column, 512), 512)
        copies.append(pltpu.make_async_copy(work_ref.at[i], out_ref.at[:, columns], sems.at[i]))
        copies[-1].start()
    return copies


def project_kernel(apart, bits_ref, inverse_ref, *refs):
    out_ref, work_ref, sems = refs[-3:]
    for copy in project_columns(apart, bits_ref, inverse_ref, refs[: len(apart)], out_ref, work_ref, sems):
        copy.wait()


def basis_kernel(apart, bits_ref, inverse_ref, *refs):
    sampled_ref = refs[len(apart)]
    out_ref, basis_ref, work_ref, rows_ref, sems = refs[-5:]
    copies = project_columns(apart, bits_ref, inverse_ref, refs[: len(apart)], out_ref, work_ref, sems)
    rows_ref[...] = lax.dot_general(
        sampled_ref[...],
        inverse_ref[...],
        (((1,), (1,)), ((), ())),
        precision=lax.Precision.HIGHEST,
        preferred_element_type=F32,
    )
    last = pltpu.make_async_copy(rows_ref, basis_ref, sems.at[len(apart)])
    last.start()
    for copy in copies:
        copy.wait()
    last.wait()


def project(bits, inverse, sources, apart, sampled=None, into=None):
    whole = pl.BlockSpec(memory_space=pltpu.VMEM)
    away = pl.BlockSpec(memory_space=pl.ANY)
    operands, in_specs = [inverse, *sources], [whole] * (1 + len(sources))
    out_shape = [jax.ShapeDtypeStruct((K, D), F32)]
    scratch = [pltpu.VMEM((len(sources), K, 512), F32)]
    if sampled is not None:
        operands.append(sampled)
        in_specs.append(whole)
        out_shape.append(jax.ShapeDtypeStruct((ROWS_DEV, K), F32))
        scratch.append(pltpu.VMEM((ROWS_DEV, K), F32))
    if into is not None:
        operands.append(into)
        in_specs.append(away)
    kernel = project_kernel if sampled is None else basis_kernel
    return pl.pallas_call(
        functools.partial(kernel, apart),
        grid_spec=pltpu.PrefetchScalarGridSpec(
            num_scalar_prefetch=1,
            grid=(),
            in_specs=in_specs,
            out_specs=[away] * len(out_shape),
            scratch_shapes=scratch + [pltpu.SemaphoreType.DMA((len(sources) + 1,))],
        ),
        out_shape=out_shape,
        input_output_aliases={} if into is None else {len(operands): 0},
        compiler_params=PARAMS,
        cost_estimate=pl.CostEstimate(
            flops=6 * K * K * 512 * len(sources), bytes_accessed=4_000_000, transcendentals=0
        ),
        name=f"project{len(sources)}",
    )(bits, *operands)


WAYS = ({"x": 1}, {"x": -1}, {"y": 1}, {"y": -1})


def shards(corpus, sketch):
    bits = own_bits()
    corpus, sampled, both, gram, away = sketch_rows(bits, corpus, sketch)

    far_received = shift(away, core=1)
    far, near_away = correlate(bits, corpus, both, gram, ((0, 1), (1, 0)))
    near_received = shift(near_away, core=1)
    (near,) = correlate(bits, corpus, both, gram, ((0, 0),))
    with jax.named_scope("scatter_neighbours"):
        rows = [slice(SEND * d, SEND * d + SEND) for d in range(4)]
        sent = [shift(far[rows[d]] + far_received[rows[d]], **WAYS[d]) for d in range(4)]
        parts = merge(bits, near, near_received, far, far_received, sent)
    with jax.named_scope("scatter_rest"):
        own = total(bits, exchange(parts, 2))
    with jax.named_scope("total_z"):
        four = shift(own, z=4)
        two, six = shift(own, z=2), shift(own, z=6)
        own = (own + four) + (two + six)

    with jax.named_scope("gather_rest"):
        near = exchange(jnp.broadcast_to(own[None], (8, PART, 128)), 1)
    with jax.named_scope("gather_gram"):
        gram_own = near[:, 128:, :]
        gram_other = shift(gram_own, core=1)
    with jax.named_scope("gather_neighbours"):
        rows = near[:, 0:128, :]
        far = [shift(rows, y=1, z=-1), shift(rows, x=1), shift(rows, z=1)]
    near_late, gram_other = lax.optimization_barrier((near, gram_other))
    with jax.named_scope("gather_core"):
        near_other = shift(near_late, core=1)
    inverse = inverse_factor(bits, gram_own, gram_other)
    quarters = ((1, 1), (1, 0), (0, 1))
    projected, basis = project(
        bits, inverse, (near, near_other), ((0, 0, 0), (1, 0, 0)), sampled=sampled
    )
    *far, projected = lax.optimization_barrier((*far, projected))
    with jax.named_scope("gather_core"):
        far_other = [shift(part, core=1) for part in far]
    (projected,) = project(bits, inverse, far, tuple((0, *q) for q in quarters), into=projected)
    (projected,) = project(bits, inverse, far_other, tuple((1, *q) for q in quarters), into=projected)
    return (basis, projected)


def solution(mesh):
    return jax.shard_map(
        shards,
        mesh=mesh,
        in_specs=(P(AXES, None), P()),
        out_specs=(P(AXES, None), P()),
        check_vma=False,
    )
```

```python
import functools

import jax
import jax.numpy as jnp
from jax import lax
from jax.experimental import pallas as pl
from jax.experimental.pallas import tpu as pltpu
from jax.sharding import PartitionSpec as P

AXES = ("rowa", "rowb")
D = 4096
K = 256
ROWS_DEV = 768
ROWS = 196608
NX, NY, NZ = 4, 4, 8
F32 = jnp.float32
BF16 = jnp.bfloat16
PART = 160
KEEP, SEND = 512, 640
PARAMS = pltpu.CompilerParams(vmem_limit_bytes=24 * 1024 * 1024)


def index_of(x, y, z, core):
    return ((x % 2) * 16 + z * 2 + core) * 8 + (x // 2) * 4 + y


def shift(value, x=0, y=0, z=0, core=0):
    pairs = [
        (index_of(i, j, k, c), index_of((i + x) % NX, (j + y) % NY, (k + z) % NZ, (c + core) % 2))
        for i in range(NX)
        for j in range(NY)
        for k in range(NZ)
        for c in range(2)
    ]
    return lax.ppermute(value, AXES, pairs)


def exchange(value, planes):
    groups = [
        [
            index_of((2 * u + j % 2 - s) % NX, j, planes * k + p, c)
            for p in range(planes)
            for j in range(NY)
            for u in range(2)
        ]
        for s in range(2)
        for k in range(NZ // planes)
        for c in range(2)
    ]
    return lax.all_to_all(value, AXES, 0, 0, axis_index_groups=groups, tiled=True)


def own_bits():
    a, b = lax.axis_index("rowa"), lax.axis_index("rowb")
    return jnp.stack([a % 2, (a // 16 + b) % 2, (b // 2) % 2, (a // 2) % 2]).astype(jnp.int32)


def split(value):
    high = value.astype(BF16)
    return high, (value - high.astype(F32)).astype(BF16)


CHUNKS = 4


def sketch_kernel(bits_ref, corpus_ref, sketch_ref, rows_ref, sampled_ref, both_ref, gram_ref, away_ref, sems):
    chunk = D // CHUNKS
    copies = []
    for k in range(CHUNKS):
        span = pl.ds(k * chunk, chunk)
        copies.append(pltpu.make_async_copy(corpus_ref.at[:, span], rows_ref.at[:, span], sems.at[k]))
    for copy in copies:
        copy.start()
    for k, copy in enumerate(copies):
        copy.wait()
        span = slice(k * chunk, (k + 1) * chunk)
        part = jnp.dot(rows_ref[:, span], sketch_ref[span, :], preferred_element_type=F32)
        sampled_ref[...] = part if k == 0 else sampled_ref[...] + part
    rest = []
    for k in range(ROWS_DEV // K):
        turned = sampled_ref[k * K : (k + 1) * K, :].T
        high, low = split(turned)
        both_ref[0:K, k * K : (k + 1) * K] = high
        both_ref[K:, k * K : (k + 1) * K] = low
        rest.append((turned - high.astype(F32) - low.astype(F32)).astype(BF16))
    rest = jnp.concatenate(rest, axis=1)
    high, low = both_ref[0:K, :], both_ref[K:, :]
    across = functools.partial(
        lax.dot_general, dimension_numbers=(((1,), (1,)), ((), ())), preferred_element_type=F32
    )
    mirrored = across(rest, high) + across(low, high)
    gram_ref[...] = (mirrored + mirrored.T + across(low, low)) + across(high, high)
    correlate_kernel(1, 1, bits_ref, rows_ref, both_ref, gram_ref, away_ref)


def sketch_rows(bits, corpus, sketch):
    return pl.pallas_call(
        sketch_kernel,
        grid_spec=pltpu.PrefetchScalarGridSpec(
            num_scalar_prefetch=1,
            grid=(),
            in_specs=[pl.BlockSpec(memory_space=pl.ANY), pl.BlockSpec(memory_space=pltpu.VMEM)],
            out_specs=[pl.BlockSpec(memory_space=pltpu.VMEM)] * 5,
            scratch_shapes=[pltpu.SemaphoreType.DMA((CHUNKS,))],
        ),
        out_shape=[
            jax.ShapeDtypeStruct((ROWS_DEV, D), BF16),
            jax.ShapeDtypeStruct((ROWS_DEV, K), F32),
            jax.ShapeDtypeStruct((2 * K, ROWS_DEV), BF16),
            jax.ShapeDtypeStruct((K, K), F32),
            jax.ShapeDtypeStruct((4 * SEND, 128), F32),
        ],
        compiler_params=pltpu.CompilerParams(vmem_limit_bytes=40 * 1024 * 1024),
        cost_estimate=pl.CostEstimate(
            flops=3 * ROWS_DEV * D * K, bytes_accessed=9_000_000, transcendentals=0
        ),
        name="sketch_rows",
    )(bits, corpus, sketch)


def correlate_kernel(flip, leaves, bits_ref, corpus_ref, both_ref, gram_ref, out_ref):
    core = bits_ref[0] ^ flip
    start = core * 2048 + (bits_ref[1] ^ leaves) * 1024
    size = SEND if leaves else KEEP
    for i in range(4):
        columns = pl.ds(pl.multiple_of(start + 256 * i, 256), 256)
        part = jnp.dot(both_ref[...], corpus_ref[:, columns], preferred_element_type=F32)
        part = part[0:K] + part[K:]
        for q in range(4):
            row = size * i + 128 * q
            out_ref[row : row + 64, :] = part[64 * q : 64 * q + 64, 0:128]
            out_ref[row + 64 : row + 128, :] = part[64 * q : 64 * q + 64, 128:256]
        if leaves:
            lanes = pl.ds(pl.multiple_of(core * 128, 128), 128)
            out_ref[size * i + 512 : size * i + 640, :] = gram_ref[128 * (i // 2) : 128 * (i // 2) + 128, lanes]


def correlate_some_kernel(which, bits_ref, corpus_ref, both_ref, gram_ref, *out_refs):
    for (flip, leaves), out_ref in zip(which, out_refs):
        correlate_kernel(flip, leaves, bits_ref, corpus_ref, both_ref, gram_ref, out_ref)


def correlate(bits, corpus, both, gram, which):
    return pl.pallas_call(
        functools.partial(correlate_some_kernel, which),
        grid_spec=pltpu.PrefetchScalarGridSpec(
            num_scalar_prefetch=1,
            grid=(),
            in_specs=[pl.BlockSpec(memory_space=pltpu.VMEM)] * 3,
            out_specs=[pl.BlockSpec(memory_space=pltpu.VMEM)] * len(which),
        ),
        out_shape=[
            jax.ShapeDtypeStruct((4 * (SEND if leaves else KEEP), 128), F32) for _, leaves in which
        ],
        compiler_params=PARAMS,
        cost_estimate=pl.CostEstimate(
            flops=ROWS_DEV * D * K * len(which), bytes_accessed=3_000_000, transcendentals=0
        ),
        name=f"correlate{len(which)}",
    )(bits, corpus, both, gram)


def merge_kernel(bits_ref, kept_ref, received_ref, gram_ref, gram_received_ref, *refs):
    out_ref = refs[4]
    even = bits_ref[1] == 0
    for m in range(16):
        d, q = m // 4, m % 4
        rows = slice(128 * m, 128 * m + 128)
        out_ref[m, 0:128, :] = kept_ref[rows, :] + received_ref[rows, :] + refs[d][128 * q : 128 * q + 128, :]
        way = 2 * (m % 8 // 4)
        row = 512 + 32 * (m % 4)
        own = slice(SEND * way + row, SEND * way + row + 32)
        other = jnp.where(even, refs[way][row : row + 32, :], refs[way + 1][row : row + 32, :])
        out_ref[m, 128:160, :] = (gram_ref[own, :] + gram_received_ref[own, :]) + other


def merge(bits, kept, received, gram, gram_received, sent):
    return pl.pallas_call(
        merge_kernel,
        grid_spec=pltpu.PrefetchScalarGridSpec(
            num_scalar_prefetch=1,
            grid=(),
            in_specs=[pl.BlockSpec(memory_space=pltpu.VMEM)] * 8,
            out_specs=pl.BlockSpec(memory_space=pltpu.VMEM),
        ),
        out_shape=jax.ShapeDtypeStruct((16, PART, 128), F32),
        compiler_params=PARAMS,
        name="merge",
    )(bits, kept, received, gram, gram_received, *sent)


def total_kernel(bits_ref, parts_ref, out_ref):
    order = [8 * p + 2 * ((j - 1) % 4) + (u ^ (j % 2)) for p in range(2) for j in range(4) for u in range(2)]
    out_ref[...] = functools.reduce(jnp.add, [parts_ref[m] for m in range(16)])

    @pl.when(bits_ref[1] * bits_ref[2] == 1)
    def _():
        out_ref[128:160, :] = functools.reduce(jnp.add, [parts_ref[m, 128:160, :] for m in order])


def total(bits, parts):
    return pl.pallas_call(
        total_kernel,
        grid_spec=pltpu.PrefetchScalarGridSpec(
            num_scalar_prefetch=1,
            grid=(),
            in_specs=[pl.BlockSpec(memory_space=pltpu.VMEM)],
            out_specs=pl.BlockSpec(memory_space=pltpu.VMEM),
        ),
        out_shape=jax.ShapeDtypeStruct((PART, 128), F32),
        compiler_params=PARAMS,
        name="total",
    )(bits, parts)


def eliminate(panel, start):
    count = panel.shape[0] // 8
    lanes = lax.broadcasted_iota(jnp.int32, (8, K), 1)
    below = lax.broadcasted_iota(jnp.int32, (8, K), 0)
    row_of = lax.broadcasted_iota(jnp.int32, (8, 128), 0)
    tiles = [panel[8 * t : 8 * t + 8, :] for t in range(count)]
    for b in range(count):
        first = start + 8 * b
        columns = [
            [jnp.broadcast_to(tiles[t][:, first + k : first + k + 1], (8, 128)) for t in range(b, count)]
            for k in range(8)
        ]
        own = jnp.logical_and(lanes >= first, lanes < first + 8)
        for t in range(b, count):
            fresh = jnp.where(lanes - first == below, 1.0, 0.0) if t == b else 0.0
            tiles[t] = jnp.where(own, fresh, tiles[t])
        pivots = jnp.ones((8, 128), F32)
        for j in range(8):
            lead = columns[j][0]
            pivot = jnp.broadcast_to(lead[j : j + 1, :], (8, 128))
            pivots = jnp.where(row_of == j, pivot, pivots)
            inverse = 1.0 / pivot
            row = tiles[b][j : j + 1, :]
            across = [jnp.broadcast_to(lead[k : k + 1, :], (8, 128)) for k in range(8)]
            for t in range(b, count):
                factor = columns[j][t - b] * inverse
                if t == b:
                    factor = jnp.where(row_of > j, factor, 0.0)
                for k in range(j + 1, 8):
                    columns[k][t - b] = columns[k][t - b] - factor * across[k]
                tiles[t] = tiles[t] - jnp.concatenate([factor, factor], axis=1) * row
        scale = lax.rsqrt(pivots)
        tiles[b] = tiles[b] * jnp.concatenate([scale, scale], axis=1)
    return jnp.concatenate(tiles, axis=0)


def factor_kernel(bits_ref, own_ref, other_ref, out_ref, half_ref, work_ref):
    for m in range(8):
        half_ref[bits_ref[0], 32 * m : 32 * m + 32, :] = own_ref[m]
        half_ref[1 - bits_ref[0], 32 * m : 32 * m + 32, :] = other_ref[m]
    work_ref[:, 0:128] = half_ref[0] / ROWS
    work_ref[:, 128:256] = half_ref[1] / ROWS
    step = 64
    lanes = lax.broadcasted_iota(jnp.int32, (1, K), 1)
    rows = lax.broadcasted_iota(jnp.int32, (step, 1), 0)
    for start in range(0, K, step):
        panel = eliminate(work_ref[start : start + step, :], start)
        end = start + step
        out_ref[start:end, :] = jnp.where(lanes <= rows + start, panel, 0.0)
        own = jnp.logical_and(lanes >= start, lanes < end)
        masked = jnp.where(jnp.logical_and(own, lanes - start > rows), 0.0, panel)
        if end < K:
            update = lax.dot_general(
                panel[:, end:],
                masked,
                (((0,), (0,)), ((), ())),
                precision=lax.Precision.HIGHEST,
                preferred_element_type=F32,
            )
            work_ref[end:, :] = jnp.where(own, 0.0, work_ref[end:, :]) - update


def inverse_factor(bits, own, other):
    return pl.pallas_call(
        factor_kernel,
        grid_spec=pltpu.PrefetchScalarGridSpec(
            num_scalar_prefetch=1,
            grid=(),
            in_specs=[pl.BlockSpec(memory_space=pltpu.VMEM)] * 2,
            out_specs=pl.BlockSpec(memory_space=pltpu.VMEM),
            scratch_shapes=[pltpu.VMEM((2, K, 128), F32), pltpu.VMEM((K, K), F32)],
        ),
        out_shape=jax.ShapeDtypeStruct((K, K), F32),
        compiler_params=PARAMS,
        cost_estimate=pl.CostEstimate(
            flops=10_000_000_000, bytes_accessed=1_000_000, transcendentals=0
        ),
        name="inverse_factor",
    )(bits, own, other)


def project_columns(apart, bits_ref, inverse_ref, sources, out_ref, work_ref, sems):
    inverse_high, inverse_low = split(inverse_ref[...])
    both = jnp.concatenate([inverse_high, inverse_low], axis=0)
    copies = []
    for i, source in enumerate(sources):
        rows = [
            jnp.concatenate([source[4 * h + q, a : a + 64, :] for h in range(2) for a in (0, 64)], axis=1)
            for q in range(4)
        ]
        high, low = split(jnp.concatenate(rows, axis=0))
        part = jnp.dot(both, high, preferred_element_type=F32)
        part = jnp.dot(inverse_high, low, preferred_element_type=F32) + part[K:] + part[0:K]
        work_ref[i] = part * (1.0 / ROWS**0.5)
        core, plane, level = apart[i]
        column = (bits_ref[0] ^ core) * 2048 + (bits_ref[1] ^ plane) * 1024 + (bits_ref[3] ^ level) * 512
        columns = pl.ds(pl.multiple_of(column, 512), 512)
        copies.append(pltpu.make_async_copy(work_ref.at[i], out_ref.at[:, columns], sems.at[i]))
        copies[-1].start()
    return copies


def project_kernel(apart, bits_ref, inverse_ref, *refs):
    out_ref, work_ref, sems = refs[-3:]
    for copy in project_columns(apart, bits_ref, inverse_ref, refs[: len(apart)], out_ref, work_ref, sems):
        copy.wait()


def basis_kernel(apart, bits_ref, inverse_ref, *refs):
    sampled_ref = refs[len(apart)]
    out_ref, basis_ref, work_ref, rows_ref, sems = refs[-5:]
    copies = project_columns(apart, bits_ref, inverse_ref, refs[: len(apart)], out_ref, work_ref, sems)
    rows_ref[...] = lax.dot_general(
        sampled_ref[...],
        inverse_ref[...],
        (((1,), (1,)), ((), ())),
        precision=lax.Precision.HIGHEST,
        preferred_element_type=F32,
    )
    last = pltpu.make_async_copy(rows_ref, basis_ref, sems.at[len(apart)])
    last.start()
    for copy in copies:
        copy.wait()
    last.wait()


def project(bits, inverse, sources, apart, sampled=None, into=None):
    whole = pl.BlockSpec(memory_space=pltpu.VMEM)
    away = pl.BlockSpec(memory_space=pl.ANY)
    operands, in_specs = [inverse, *sources], [whole] * (1 + len(sources))
    out_shape = [jax.ShapeDtypeStruct((K, D), F32)]
    scratch = [pltpu.VMEM((len(sources), K, 512), F32)]
    if sampled is not None:
        operands.append(sampled)
        in_specs.append(whole)
        out_shape.append(jax.ShapeDtypeStruct((ROWS_DEV, K), F32))
        scratch.append(pltpu.VMEM((ROWS_DEV, K), F32))
    if into is not None:
        operands.append(into)
        in_specs.append(away)
    kernel = project_kernel if sampled is None else basis_kernel
    return pl.pallas_call(
        functools.partial(kernel, apart),
        grid_spec=pltpu.PrefetchScalarGridSpec(
            num_scalar_prefetch=1,
            grid=(),
            in_specs=in_specs,
            out_specs=[away] * len(out_shape),
            scratch_shapes=scratch + [pltpu.SemaphoreType.DMA((len(sources) + 1,))],
        ),
        out_shape=out_shape,
        input_output_aliases={} if into is None else {len(operands): 0},
        compiler_params=PARAMS,
        cost_estimate=pl.CostEstimate(
            flops=6 * K * K * 512 * len(sources), bytes_accessed=4_000_000, transcendentals=0
        ),
        name=f"project{len(sources)}",
    )(bits, *operands)


WAYS = ({"x": 1}, {"x": -1}, {"y": 1}, {"y": -1})


def shards(corpus, sketch):
    bits = own_bits()
    corpus, sampled, both, gram, away = sketch_rows(bits, corpus, sketch)

    far_received = shift(away, core=1)
    far, near_away = correlate(bits, corpus, both, gram, ((0, 1), (1, 0)))
    near_received = shift(near_away, core=1)
    (near,) = correlate(bits, corpus, both, gram, ((0, 0),))
    with jax.named_scope("scatter_neighbours"):
        rows = [slice(SEND * d, SEND * d + SEND) for d in range(4)]
        sent = [shift(far[rows[d]] + far_received[rows[d]], **WAYS[d]) for d in range(4)]
        parts = merge(bits, near, near_received, far, far_received, sent)
    with jax.named_scope("scatter_rest"):
        own = total(bits, exchange(parts, 2))
    with jax.named_scope("total_z"):
        four = shift(own, z=4)
        two, six = shift(own, z=2), shift(own, z=6)
        own = (own + four) + (two + six)

    with jax.named_scope("gather_rest"):
        near = exchange(jnp.broadcast_to(own[None], (8, PART, 128)), 1)
    with jax.named_scope("gather_gram"):
        gram_own = near[:, 128:, :]
        gram_other = shift(gram_own, core=1)
    with jax.named_scope("gather_neighbours"):
        rows = near[:, 0:128, :]
        far = [shift(rows, y=1, z=-1), shift(rows, x=1), shift(rows, z=1)]
    near_late, gram_other = lax.optimization_barrier((near, gram_other))
    with jax.named_scope("gather_core"):
        near_other = shift(near_late, core=1)
    inverse = inverse_factor(bits, gram_own, gram_other)
    quarters = ((1, 1), (1, 0), (0, 1))
    projected, basis = project(
        bits, inverse, (near, near_other), ((0, 0, 0), (1, 0, 0)), sampled=sampled
    )
    *far, projected = lax.optimization_barrier((*far, projected))
    with jax.named_scope("gather_core"):
        far_other = [shift(part, core=1) for part in far]
    (projected,) = project(bits, inverse, far, tuple((0, *q) for q in quarters), into=projected)
    (projected,) = project(bits, inverse, far_other, tuple((1, *q) for q in quarters), into=projected)
    return (basis, projected)


def solution(mesh):
    return jax.shard_map(
        shards,
        mesh=mesh,
        in_specs=(P(AXES, None), P()),
        out_specs=(P(AXES, None), P()),
        check_vma=False,
    )
```
